256 devices in a mesh: dp: 64 (over x_hi, z, y), pair: 4 (over x_lo, core).
Axes of the slice: x: 4 (x_hi: 2, x_lo: 2; x = x_hi * 2 + x_lo), y: 4, z: 8, core: 2. Of those that a mesh axis runs over, the one named last changes fastest.
Arguments:
- image_feats: bfloat16 [65536, 1152], P(('dp', 'pair')), may hold values from -24 to 24
- text_feats: bfloat16 [65536, 1152], P(('dp', 'pair')), may hold values from -24 to 24
- image_head: bfloat16 [1152, 1152], replicated, may hold values from -0.1875 to 0.1875
- text_head: bfloat16 [1152, 1152], replicated, may hold values from -0.1875 to 0.1875
- logit_scale: float32 [1], replicated, may hold values from 4 to 16
- logit_bias: float32 [1], replicated, may hold values from -3 to -1
Outputs:
- image_grads: bfloat16 [65536, 1152], P(('dp', 'pair'))
- text_grads: bfloat16 [65536, 1152], P(('dp', 'pair'))
- head_grads: float32 [1152, 2304], P('pair')
The draws below stay inside these ranges and needn't reach their ends.
All inputs are finite; a program needn't handle non-finite values.
Results may differ from the reference program's by a relative error of at most 0.008.
Values may be sent and summed in bfloat16 or wider, within the bound.
No kernel may reach another device: no remote copies, remote signals or barrier semaphores. Data moves between devices by JAX's collectives and lax.ppermute only.
A program may use at most 128 MiB of HBM per device.

```python
import math
import jax
import jax.numpy as jnp
from jax import lax

D = 1152
E = 1152
GROUP = 1024
TOKENS = 65536
N_DP = 64
N_PAIR = 4


def with_spikes(array, key, source, target, parts, factor):
    def block_of(axis_at):
        return (jnp.arange(array.shape[axis_at]) // (array.shape[axis_at] // parts)).reshape((-1,) + (1,) * (array.ndim - 1 - axis_at))

    near = jax.random.permutation(key, parts)[block_of(target)]
    far = (block_of(target) + parts // 2) % parts
    return jnp.where((block_of(source) == near) | (block_of(source) == far), factor * array, array)


def shard_levels(stream_key, dims, split, smallest, top_value):
    level = 1.0
    for axis_at, shards_of in split:
        steps = jax.random.uniform(jax.random.fold_in(jax.random.fold_in(stream_key, 6), axis_at), (shards_of,), jnp.float32, smallest / len(split), top_value / len(split))
        level = level * jnp.repeat(jnp.exp(steps), dims[axis_at] // shards_of).reshape((-1,) + (1,) * (len(dims) - 1 - axis_at))
    return level


def scatter_about(rng, extent, width, reach, pieces=(), kind=jnp.bfloat16):
    drawn = jax.random.normal(rng, extent, jnp.float32) * width
    if len(pieces) > 0:
        drawn = shard_levels(rng, extent, pieces, -0.22, 0.18) * drawn
    return jnp.clip(drawn, min=-reach, max=reach).astype(kind)


def noise_with(key, extent, spread, limit, shards, heavy, kind=jnp.bfloat16):
    entries = spread * jax.random.normal(key, extent, jnp.float32)
    if shards:
        entries = entries * shard_levels(key, extent, shards, -0.22, 0.18)
    return jnp.clip(with_spikes(entries, jax.random.fold_in(key, 3), *heavy), -limit, limit).astype(kind)


def setup_inputs(seed: int = 0) -> dict:
    splits = jax.random.split(jax.random.key(seed), 7)
    return {
        "image_feats": noise_with(splits[0], (TOKENS, D), 1.0, 24.0, ((0, 256),), (0, 1, 128, 5.5)),
        "text_feats": noise_with(splits[1], (TOKENS, D), 1.0, 24.0, ((0, 256),), (0, 1, 128, 5.5)),
        "image_head": scatter_about(splits[2], (D, E), D ** -0.5, 0.1875),
        "text_head": scatter_about(splits[3], (D, E), D ** -0.5, 0.1875),
        "logit_scale": jnp.clip(jnp.exp(jax.random.uniform(splits[4], (1,), jnp.float32, math.log(4.0), math.log(16.0))), 4.0, 16.0),
        "logit_bias": jnp.clip(jax.random.uniform(splits[5], (1,), jnp.float32, -3.0, -1.0), -3.0, -1.0),
    }


def embed(feats, weight):
    u = jnp.dot(feats, weight, preferred_element_type=jnp.float32)
    inv = lax.rsqrt(lax.optimization_barrier(jnp.sum(u * u, axis=1, keepdims=True)) + 1e-06)
    return (u * inv, inv)

def tile_weights(img, txt, scale, bias, positive):
    logits = scale * lax.dot_general(img, txt, (((1,), (1,)), ((), ())), preferred_element_type=jnp.float32) + bias
    sign = jnp.where(positive, 1.0, -1.0).astype(jnp.float32)
    deriv = -sign * jax.nn.sigmoid(-sign * logits)
    return (scale * deriv).astype(jnp.bfloat16)

def backward(z_val, inv, dz_val):
    return (inv * (dz_val - z_val * lax.optimization_barrier(jnp.sum(z_val * dz_val, axis=1, keepdims=True)))).astype(jnp.bfloat16)

def reference(image_feats, text_feats, image_head, text_head, logit_scale, logit_bias):
    z_img, inv_img = embed(image_feats, image_head)
    z_txt, inv_txt = embed(text_feats, text_head)
    imgs = z_img.astype(jnp.bfloat16).reshape(N_DP, GROUP, E)
    txts = z_txt.astype(jnp.bfloat16).reshape(N_DP, GROUP, E)
    scale = logit_scale[0]
    bias = logit_bias[0]
    eye = jnp.eye(GROUP, dtype=jnp.int32) > 0
    masks = [0, N_DP // 2, N_DP // 4]

    def per_group(index):
        own_img = imgs[index]
        own_txt = txts[index]
        dz_i = jnp.zeros((GROUP, E), jnp.float32)
        dz_t = jnp.zeros((GROUP, E), jnp.float32)
        for flip in masks:
            other = jnp.bitwise_xor(index, jnp.int32(flip)).astype(jnp.int32)
            positive = eye if flip == 0 else jnp.zeros((GROUP, GROUP), bool)
            w_img = tile_weights(own_img, txts[other], scale, bias, positive)
            dz_i = dz_i + jnp.dot(w_img, txts[other], preferred_element_type=jnp.float32)
            w_txt = tile_weights(imgs[other], own_txt, scale, bias, positive)
            dz_t = dz_t + lax.dot_general(w_txt, imgs[other], (((0,), (0,)), ((), ())), preferred_element_type=jnp.float32)
        return (dz_i, dz_t)
    dz_img, dz_txt = lax.map(per_group, jnp.arange(N_DP, dtype=jnp.int32))
    dz_img = dz_img.reshape(TOKENS, E)
    dz_txt = dz_txt.reshape(TOKENS, E)
    du_img = backward(z_img, inv_img, dz_img)
    du_txt = backward(z_txt, inv_txt, dz_txt)
    contract = (((1,), (1,)), ((), ()))
    image_grads = lax.dot_general(du_img, image_head, contract, preferred_element_type=jnp.float32).astype(jnp.bfloat16)
    text_grads = lax.dot_general(du_txt, text_head, contract, preferred_element_type=jnp.float32).astype(jnp.bfloat16)
    rows = (((0,), (0,)), ((), ()))
    head_img = lax.dot_general(image_feats, du_img, rows, preferred_element_type=jnp.float32)
    head_txt = lax.dot_general(text_feats, du_txt, rows, preferred_element_type=jnp.float32)
    head_grads = jnp.concatenate([head_img, head_txt], axis=1) / (N_DP * N_PAIR)
    return (image_grads, text_grads, head_grads)
```

```python
import jax
import jax.numpy as jnp
from jax import lax
from jax.sharding import Mesh, PartitionSpec as P

ROWS = ("xh", "z", "y", "xl", "c")
X_RING = ("xh", "xl")
SWAP = [(0, 1), (1, 0)]
CROSS = [(0, 3), (3, 0), (1, 2), (2, 1)]
F32 = jnp.float32
BF16 = jnp.bfloat16


def ring(count, step):
    return [(i, (i + step) % count) for i in range(count)]


def far_z(block):
    count = lax.axis_size("z")
    parts = jnp.split(block, 4, axis=0)
    out = []
    for i, part in enumerate(parts):
        step = 2 if i % 2 == 0 else -2
        part = lax.ppermute(part, "z", ring(count, step))
        out.append(lax.ppermute(part, "z", ring(count, step)))
    return out


def embed(feats, weight):
    u = jnp.dot(feats, weight, preferred_element_type=F32)
    inv = lax.rsqrt(jnp.sum(u * u, axis=1, keepdims=True) + 1e-06)
    return (u * inv, inv)


def tile_weights(txt, img, scale, bias, positive):
    logits = (
        scale
        * lax.dot_general(txt, img, (((1,), (1,)), ((), ())), preferred_element_type=F32)
        + bias
    )
    if positive is None:
        deriv = jax.nn.sigmoid(logits)
    else:
        sign = jnp.where(positive, 1.0, -1.0).astype(F32)
        deriv = -sign * jax.nn.sigmoid(-sign * logits)
    return (scale * deriv).astype(BF16)


def over_rows(a, b):
    return lax.dot_general(a, b, (((0,), (0,)), ((), ())), preferred_element_type=F32)


def backward(z_val, inv, dz_val):
    return (inv * (dz_val - z_val * jnp.sum(z_val * dz_val, axis=1, keepdims=True))).astype(BF16)


def spread(piece, axes):
    count = lax.axis_size(axes)
    return lax.all_to_all(
        jnp.broadcast_to(piece[None], (count,) + piece.shape), axes, 0, 0, tiled=True
    )


def per_device(image_feats, text_feats, image_head, text_head, logit_scale, logit_bias):
    rows = image_feats.shape[0]
    scale = logit_scale[0]
    bias = logit_bias[0]
    core = lax.axis_index("c")

    z_txt, inv_txt = embed(text_feats, text_head)
    zb_txt = z_txt.astype(BF16)
    far = far_z(zb_txt)
    near = lax.ppermute(zb_txt, X_RING, CROSS)

    z_img, inv_img = embed(image_feats, image_head)
    zb_img = z_img.astype(BF16)
    next_img = lax.ppermute(zb_img, "xl", SWAP)
    core_img = lax.ppermute(zb_img, "c", SWAP)
    next_core_img = lax.ppermute(next_img, "c", SWAP)
    imgs = jnp.concatenate([zb_img, core_img, next_img, next_core_img], axis=0)

    depth = image_feats.shape[1]
    block = depth // 4

    def halves(feats):
        cut = feats.reshape(rows, 2, 2, block)
        mine = lax.dynamic_index_in_dim(cut, core, 2, keepdims=False).reshape(rows, 2 * block)
        other = lax.dynamic_index_in_dim(cut, 1 - core, 2, keepdims=False).reshape(rows, 2 * block)
        return jnp.concatenate([mine, lax.ppermute(other, "c", SWAP)], axis=0)

    img_cols = halves(image_feats)
    txt_cols = halves(text_feats)

    row_ids = lax.broadcasted_iota(jnp.int32, (rows, imgs.shape[0]), 0)
    col_ids = lax.broadcasted_iota(jnp.int32, (rows, imgs.shape[0]), 1)
    w_home = tile_weights(zb_txt, imgs, scale, bias, row_ids == col_ids)
    dz_txt = jnp.dot(w_home, imgs, preferred_element_type=F32)
    w_near = tile_weights(near, imgs, scale, bias, None)
    back_near = jnp.dot(w_near, imgs, preferred_element_type=F32).astype(BF16)
    back_near = lax.ppermute(back_near, X_RING, CROSS)
    far_all = jnp.concatenate(far, axis=0)
    w_far = tile_weights(far_all, imgs, scale, bias, None)
    back_far = jnp.dot(w_far, imgs, preferred_element_type=F32).astype(BF16)
    back_far = jnp.concatenate(far_z(back_far), axis=0)

    dz_part = over_rows(w_home, zb_txt) + over_rows(w_near, near) + over_rows(w_far, far_all)
    dz_part = dz_part.reshape(2, 2, rows, -1)
    core_part = lax.ppermute(dz_part[:, 1].astype(BF16), "c", SWAP)
    dz_part = dz_part[:, 0] + core_part.astype(F32)
    dz_img = dz_part[0] + lax.ppermute(dz_part[1].astype(BF16), "xl", SWAP).astype(F32)
    du_img = backward(z_img, inv_img, dz_img)

    dz_txt = dz_txt + back_near.astype(F32) + back_far.astype(F32)
    du_txt = backward(z_txt, inv_txt, dz_txt)

    contract = (((1,), (1,)), ((), ()))
    image_grads = lax.dot_general(du_img, image_head, contract, preferred_element_type=F32)
    text_grads = lax.dot_general(du_txt, text_head, contract, preferred_element_type=F32)

    def both(du):
        return jnp.concatenate([du, lax.ppermute(du, "c", SWAP)], axis=0)

    head = jnp.concatenate(
        [over_rows(img_cols, both(du_img)), over_rows(txt_cols, both(du_txt))], axis=1
    ).astype(BF16)
    wide = head.shape[1]
    n_xy = 4 * lax.axis_size("y")
    n_z = lax.axis_size("z")
    head = head.reshape(n_xy, -1, wide)
    head = lax.all_to_all(head, ("xl", "xh", "y"), 0, 0, tiled=True)
    head = jnp.sum(head.astype(F32), axis=0).astype(BF16)
    piece = head.reshape(n_z, -1, 128)
    piece = lax.all_to_all(piece, "z", 0, 0, tiled=True)
    piece = jnp.sum(piece.astype(F32), axis=0).astype(BF16)
    piece = spread(piece, "z").reshape(head.shape)
    total = spread(piece, ("xh", "y")).reshape(block, wide)
    head_grads = total.astype(F32) / (
        lax.axis_size(("xh", "z", "y")) * lax.axis_size(("xl", "c"))
    )
    return (image_grads.astype(BF16), text_grads.astype(BF16), head_grads)


def solution(mesh):
    fine = Mesh(mesh.devices.reshape(2, 8, 4, 2, 2), ROWS)
    split = P(ROWS, None)
    return jax.shard_map(
        per_device,
        mesh=fine,
        in_specs=(split, split, P(), P(), P(), P()),
        out_specs=(split, split, P(("xl", "c"), None)),
        check_vma=False,
    )
```

```python
import functools

import jax
import jax.numpy as jnp
from jax import lax
from jax.experimental import pallas as pl
from jax.experimental.pallas import tpu as pltpu
from jax.sharding import Mesh, PartitionSpec as P

ROWS = ("xh", "z", "y", "xl", "c")
X_RING = ("xh", "xl")
SWAP = [(0, 1), (1, 0)]
CROSS = [(0, 3), (3, 0), (1, 2), (2, 1)]
F32 = jnp.float32
BF16 = jnp.bfloat16
LANES_BOTH = (((1,), (1,)), ((), ()))
ROWS_BOTH = (((0,), (0,)), ((), ()))


def shape(dims, dtype):
    return jax.ShapeDtypeStruct(dims, dtype)


def local(kernel, outs, *args, scalars=0, scratch=(), mib=14):
    vmem = pl.BlockSpec(memory_space=pltpu.VMEM)
    smem = pl.BlockSpec(memory_space=pltpu.SMEM)
    many = isinstance(outs, (tuple, list))
    return pl.pallas_call(
        kernel,
        out_shape=outs,
        in_specs=[smem] * scalars + [vmem] * (len(args) - scalars),
        out_specs=[vmem] * len(outs) if many else vmem,
        scratch_shapes=scratch,
        compiler_params=pltpu.CompilerParams(vmem_limit_bytes=mib << 20),
        cost_estimate=pl.CostEstimate(flops=1000, bytes_accessed=1000, transcendentals=0),
    )(*args)


def embedding(feats, head):
    u = jnp.dot(feats, head, preferred_element_type=F32)
    inv = lax.rsqrt(jnp.sum(u * u, axis=1, keepdims=True) + 1e-06)
    return u * inv, inv


def tangent(z, inv, dz):
    return inv * (dz - z * jnp.sum(z * dz, axis=1, keepdims=True))


def embed_kernel(head_ref, feats_ref, z_ref, inv_ref, zb_ref):
    z, inv = embedding(feats_ref[...], head_ref[...])
    z_ref[...] = z
    inv_ref[...] = inv
    zb_ref[...] = z.astype(BF16)


def embed_other_kernel(head_ref, feats_ref, zb_ref):
    zb_ref[...] = embedding(feats_ref[...], head_ref[...])[0].astype(BF16)


def embed(head, feats):
    rows, wide = feats.shape
    outs = [shape((rows, wide), F32), shape((rows, 1), F32), shape((rows, wide), BF16)]
    return local(embed_kernel, outs, head, feats)


def embed_other(head, feats):
    return local(embed_other_kernel, shape(feats.shape, BF16), head, feats)


def weigh(scale, bias, txt, img_refs, w_ref, home):
    total = None
    for i, img_ref in enumerate(img_refs):
        img = img_ref[...]
        logits = scale * lax.dot_general(txt, img, LANES_BOTH, preferred_element_type=F32) + bias
        if home and i == 0:
            row_ids = lax.broadcasted_iota(jnp.int32, logits.shape, 0)
            col_ids = lax.broadcasted_iota(jnp.int32, logits.shape, 1)
            sign = jnp.where(row_ids == col_ids, 1.0, -1.0).astype(F32)
            deriv = -sign * jax.nn.sigmoid(-sign * logits)
        else:
            deriv = jax.nn.sigmoid(logits)
        w = (scale * deriv).astype(BF16)
        w_ref[i] = w
        part = jnp.dot(w, img, preferred_element_type=F32)
        total = part if total is None else total + part
    return total


def home_first_kernel(scale_ref, bias_ref, feats_ref, head_ref, *refs):
    img_refs, (zb_ref, z_ref, inv_ref, w_ref, dz_ref) = refs[:-5], refs[-5:]
    z, inv = embedding(feats_ref[...], head_ref[...])
    txt = z.astype(BF16)
    z_ref[...] = z
    inv_ref[...] = inv
    zb_ref[...] = txt
    dz_ref[...] = weigh(scale_ref[0], bias_ref[0], txt, img_refs, w_ref, True)


def home_first(scale, bias, feats, head, imgs):
    rows, wide = feats.shape
    outs = [
        shape((rows, wide), BF16),
        shape((rows, wide), F32),
        shape((rows, 1), F32),
        shape((len(imgs), rows, imgs[0].shape[0]), BF16),
        shape((rows, wide), F32),
    ]
    return local(home_first_kernel, outs, scale, bias, feats, head, *imgs, scalars=2)


def home_rest_kernel(scale_ref, bias_ref, zb_ref, z_ref, inv_ref, part_ref, *refs):
    img_refs, (w_ref, dz_ref, du_ref) = refs[:-3], refs[-3:]
    dz = part_ref[...] + weigh(scale_ref[0], bias_ref[0], zb_ref[...], img_refs, w_ref, False)
    dz_ref[...] = dz
    du_ref[...] = tangent(z_ref[...], inv_ref[...], dz).astype(BF16)


def home_rest(scale, bias, zb, z, inv, part, imgs):
    rows, wide = zb.shape
    outs = [
        shape((len(imgs), rows, imgs[0].shape[0]), BF16),
        shape((rows, wide), F32),
        shape((rows, wide), BF16),
    ]
    return local(home_rest_kernel, outs, scale, bias, zb, z, inv, part, *imgs, scalars=2)


def text_kernel(scale_ref, bias_ref, feats_ref, head_ref, *refs):
    img_refs, (zb_ref, w_ref, dz_ref, du_ref) = refs[:-4], refs[-4:]
    z, inv = embedding(feats_ref[...], head_ref[...])
    txt = z.astype(BF16)
    zb_ref[...] = txt
    dz = weigh(scale_ref[0], bias_ref[0], txt, img_refs, w_ref, False)
    dz_ref[...] = dz.astype(BF16)
    du_ref[...] = tangent(z, inv, dz).astype(BF16)


def text_block(scale, bias, feats, head, imgs):
    rows, wide = feats.shape
    block = shape((rows, wide), BF16)
    outs = [block, shape((len(imgs), rows, imgs[0].shape[0]), BF16), block, block]
    return local(text_kernel, outs, scale, bias, feats, head, *imgs, scalars=2)


def image_side_kernel(count, *refs):
    first_ref, rest_ref = refs[:2]
    w_refs, txt_refs, (keep_ref, send_ref) = refs[2 : count + 1], refs[count + 1 : -2], refs[-2:]
    for i in range(4):
        home = first_ref[i] if i < 2 else rest_ref[i - 2]
        weights = [home] + [ref[i] for ref in w_refs]
        dz = None
        for w, txt_ref in zip(weights, txt_refs):
            part = lax.dot_general(w, txt_ref[...], ROWS_BOTH, preferred_element_type=F32)
            dz = part if dz is None else dz + part
        if i % 2 == 0:
            keep_ref[i // 2] = dz
        else:
            send_ref[i // 2] = dz.astype(BF16)


def image_side(home, weights, txts):
    rows, wide = txts[0].shape
    dims = (2, rows, wide)
    return local(
        functools.partial(image_side_kernel, len(txts)),
        [shape(dims, F32), shape(dims, BF16)],
        *home,
        *weights,
        *txts,
    )


def image_tangent_kernel(keep_ref, got_ref, *refs):
    z_refs, inv_refs, (du_ref, own_ref, send_ref) = refs[:2], refs[2:4], refs[4:]
    for i in range(2):
        dz = keep_ref[i] + got_ref[i].astype(F32)
        if i == 0:
            own_ref[...] = dz
        else:
            send_ref[...] = dz.astype(BF16)
        du_ref[i] = tangent(z_refs[i][...], inv_refs[i][...], dz).astype(BF16)


def image_tangent(keep, got, zs, invs):
    dims = keep.shape[1:]
    return local(
        image_tangent_kernel,
        [shape(keep.shape, BF16), shape(dims, F32), shape(dims, BF16)],
        keep,
        got,
        *zs,
        *invs,
    )


def backward_kernel(z_ref, inv_ref, own_ref, *refs):
    dz = own_ref[...]
    for ref in refs[:-1]:
        dz = dz + ref[...].astype(F32)
    refs[-1][...] = tangent(z_ref[...], inv_ref[...], dz).astype(BF16)


def backward(z, inv, own, *parts):
    return local(backward_kernel, shape(z.shape, BF16), z, inv, own, *parts)


def head_early_kernel(count, *refs):
    total = None
    for feats_ref, du_ref in zip(refs[:count], refs[count : 2 * count]):
        part = lax.dot_general(
            feats_ref[...], du_ref[...], ROWS_BOTH, preferred_element_type=F32
        )
        total = part if total is None else total + part
    refs[-1][...] = total


def head_early(feats, dus):
    depth, wide = feats[0].shape[1], dus[0].shape[1]
    return local(
        functools.partial(head_early_kernel, len(feats)),
        shape((depth, wide), F32),
        *feats,
        *dus,
        mib=20,
    )


def head_late_kernel(core_ref, *refs):
    early, (keep_ref, send_ref, held) = refs[:-3], refs[-3:]
    if len(early[1].shape) == len(early[2].shape):
        total = early[2][...] + lax.dot_general(
            early[0][...], early[1][...], ROWS_BOTH, preferred_element_type=F32
        )
    else:
        du_ref = early[-1]
        total = None
        for i, feats_ref in enumerate(early[:-1]):
            part = lax.dot_general(
                feats_ref[...], du_ref[i], ROWS_BOTH, preferred_element_type=F32
            )
            total = part if total is None else total + part
    rows = held.shape[2]
    for k in range(4):
        held[k % 2, k // 2] = total[k * rows : (k + 1) * rows]
    core = core_ref[0]
    keep_ref[...] = held[core]
    send_ref[...] = held[1 - core].astype(BF16)


def head_late(core, *args):
    depth = args[0].shape[1]
    wide = args[-1].shape[-1]
    dims = (2, depth // 4, wide)
    return local(
        head_late_kernel,
        [shape(dims, F32), shape(dims, BF16)],
        core,
        *args,
        scalars=1,
        scratch=[pltpu.VMEM((2,) + dims, F32)],
        mib=20,
    )


def split_x_kernel(keep_ref, got_ref, out_ref):
    rows = out_ref.shape[1]
    for k in range(out_ref.shape[0]):
        at = pl.ds(k % 2 * rows, rows)
        out_ref[k] = (keep_ref[k // 2, at] + got_ref[k // 2, at].astype(F32)).astype(BF16)


def split_x(keep, got):
    _, rows, wide = keep.shape
    return local(split_x_kernel, shape((4, rows // 2, wide), BF16), keep, got)


def split_y_kernel(me_ref, keep_ref, got_ref, *refs):
    outs, held = refs[:-1], refs[-1]
    count, blocks, rows = held.shape[:3]
    total = (keep_ref[...] + got_ref[...].astype(F32)).astype(BF16)
    for b in range(blocks):
        for k in range(count):
            at = (b % 2 * count + k) * rows
            held[k, b] = total[b // 2, at : at + rows]
    for s, out_ref in enumerate(outs):
        out_ref[...] = held[lax.rem(me_ref[0] + s, count)]


def split_y(me, keep, got):
    count = lax.axis_size("y")
    _, rows, wide = keep.shape
    part = (4, rows // 2 // count, wide)
    return local(
        split_y_kernel,
        [shape(part, BF16)] * count,
        me,
        keep,
        got,
        scalars=1,
        scratch=[pltpu.VMEM((count,) + part, BF16)],
    )


def sum_kernel(*refs):
    total = refs[0][...].astype(F32)
    for ref in refs[1:-1]:
        total = total + ref[...].astype(F32)
    refs[-1][...] = total.astype(BF16)


def add_up(*parts):
    return local(sum_kernel, shape(parts[0].shape, BF16), *parts)


def sum_first_kernel(in_ref, out_ref):
    total = in_ref[0].astype(F32)
    for k in range(1, in_ref.shape[0]):
        total = total + in_ref[k].astype(F32)
    out_ref[...] = total.astype(BF16)


def add_first(parts):
    return local(sum_first_kernel, shape(parts.shape[1:], BF16), parts)


def sum_split_kernel(me_ref, in_ref, *refs):
    outs, held = refs[:-1], refs[-1]
    total = in_ref[0].astype(F32)
    for k in range(1, in_ref.shape[0]):
        total = total + in_ref[k].astype(F32)
    total = total.astype(BF16)
    count, rows = held.shape[:2]
    for k in range(count):
        held[k] = total[k * rows : (k + 1) * rows]
    for s, out_ref in enumerate(outs):
        out_ref[...] = held[lax.rem(me_ref[0] + s, count)]


def add_split(me, parts):
    count = lax.axis_size("y")
    _, rows, wide = parts.shape
    part = (rows // count, wide)
    return local(
        sum_split_kernel,
        [shape(part, BF16)] * count,
        me,
        parts,
        scalars=1,
        scratch=[pltpu.VMEM((count,) + part, BF16)],
    )


def split_z_kernel(*refs):
    out_ref, ins = refs[-1], refs[:-1]
    both = jnp.concatenate([ref[...] for ref in ins], axis=0)
    rows = out_ref.shape[1]
    for k in range(out_ref.shape[0]):
        out_ref[k] = both[k * rows : (k + 1) * rows]


def split_z(*parts):
    count = lax.axis_size("z")
    rows, wide = parts[0].shape
    dims = (count, len(parts) * rows // count, wide)
    return local(split_z_kernel, shape(dims, BF16), *parts)


def sum_spread_kernel(in_ref, out_ref):
    total = in_ref[0].astype(F32)
    for k in range(1, in_ref.shape[0]):
        total = total + in_ref[k].astype(F32)
    for k in range(out_ref.shape[0]):
        out_ref[k] = total.astype(BF16)


def sum_spread(parts):
    return local(sum_spread_kernel, shape(parts.shape, BF16), parts)


def join_z_kernel(in_ref, out_ref):
    both = jnp.concatenate([in_ref[k] for k in range(in_ref.shape[0])], axis=0)
    for k in range(out_ref.shape[0]):
        out_ref[k] = both


def join_z(pieces, copies):
    count, rows, wide = pieces.shape
    return local(join_z_kernel, shape((copies, count * rows, wide), BF16), pieces)


def finish_kernel(part, in_ref, out_ref):
    count, both, wide = in_ref.shape
    rows = both // 2
    for k in range(count):
        for j in range(2):
            out_ref[k * rows : (k + 1) * rows, j * wide : (j + 1) * wide] = (
                in_ref[k, j * rows : (j + 1) * rows].astype(F32) * part
            )


def finish(part, pieces):
    count, both, wide = pieces.shape
    return local(
        functools.partial(finish_kernel, part), shape((count * both // 2, 2 * wide), F32), pieces
    )


def grads_kernel(du_ref, head_ref, out_ref):
    out = lax.dot_general(du_ref[...], head_ref[...], LANES_BOTH, preferred_element_type=F32)
    out_ref[...] = out.astype(BF16)


def feature_grads(du, head):
    return local(grads_kernel, shape(du.shape, BF16), du, head)


def far_z(block):
    count = lax.axis_size("z")
    return lax.ppermute(block, "z", [(i, (i + count // 2) % count) for i in range(count)])


def along_y(parts):
    count = lax.axis_size("y")
    return [parts[0]] + [
        lax.ppermute(part, "y", [(i, (i + s) % count) for i in range(count)])
        for s, part in enumerate(parts)
        if s > 0
    ]


def swap(block, axes):
    return lax.all_to_all(block, axes, 0, 0, tiled=True)


def per_device(image_feats, text_feats, image_head, text_head, scale, bias):
    rows, depth = image_feats.shape
    core = lax.axis_index("c").astype(jnp.int32).reshape(1)
    me_y = lax.axis_index("y").astype(jnp.int32).reshape(1)

    def unit(work):
        def nothing():
            return jax.tree.map(lambda s: jnp.zeros(s.shape, s.dtype), jax.eval_shape(work))

        return lax.cond(scale[0] > 0, work, nothing)

    far = far_z(text_feats)

    def early_unit():
        near = lax.ppermute(text_feats, X_RING, CROSS)
        next_feats = lax.ppermute(image_feats, "xl", SWAP)
        core_feats = lax.ppermute(image_feats, "c", SWAP)
        z_img, inv_img, zb_img = embed(image_head, image_feats)
        zb_core = embed_other(image_head, core_feats)
        zb_txt, z_txt, inv_txt, w_first, part = home_first(
            scale, bias, text_feats, text_head, [zb_img, zb_core]
        )
        near, next_feats, part = lax.optimization_barrier((near, next_feats, part))
        next_core_feats = lax.ppermute(next_feats, "c", SWAP)
        z_next, inv_next, zb_next = embed(image_head, next_feats)
        zb_next_core = embed_other(image_head, next_core_feats)
        w_rest, dz_txt, du_home = home_rest(
            scale, bias, zb_txt, z_txt, inv_txt, part, [zb_next, zb_next_core]
        )
        imgs = [zb_img, zb_core, zb_next, zb_next_core]
        zb_near, w_near, back_near, du_near = text_block(scale, bias, near, text_head, imgs)
        head_txt = head_early([text_feats, near], [du_home, du_near])
        return dict(
            imgs=imgs, next_feats=next_feats, z_img=z_img, inv_img=inv_img, z_next=z_next, inv_next=inv_next,
            zb_txt=zb_txt, z_txt=z_txt, inv_txt=inv_txt, home=[w_first, w_rest], dz_txt=dz_txt,
            zb_near=zb_near, w_near=w_near, back_near=back_near, head_txt=head_txt,
        )

    got = unit(early_unit)
    far, head_txt = lax.optimization_barrier((far, got["head_txt"]))
    zb_far, w_far, back_far, du_far = text_block(scale, bias, far, text_head, got["imgs"])
    back_far = far_z(back_far)
    back_near = lax.ppermute(got["back_near"], X_RING, CROSS)
    keep, send = head_late(core, far, du_far, head_txt)
    txt = split_y(me_y, keep, lax.ppermute(send, "c", SWAP))
    txt, w_far = lax.optimization_barrier((txt, w_far))
    txt = along_y(txt)

    def image_unit():
        keep, send = image_side(
            got["home"], [got["w_near"], w_far], [got["zb_txt"], got["zb_near"], zb_far]
        )
        du_part, own, send = image_tangent(
            keep,
            lax.ppermute(send, "c", SWAP),
            [got["z_img"], got["z_next"]],
            [got["inv_img"], got["inv_next"]],
        )
        keep, part = head_late(core, image_feats, got["next_feats"], du_part)
        return own, send, split_x(keep, lax.ppermute(part, "c", SWAP))

    own, send, img = unit(image_unit)
    img = swap(img, ("xl", "xh"))
    txt = add_up(*txt)
    txt, img = lax.optimization_barrier((txt, img))
    img = add_split(me_y, img)

    def second_unit():
        both = along_y(img)
        return split_z(add_up(*both), add_first(swap(txt, ("xl", "xh"))))

    piece = unit(second_unit)
    back_img = lax.ppermute(send, "xl", SWAP)
    piece, back_far, back_near = lax.optimization_barrier((piece, back_far, back_near))
    piece = swap(piece, "z")
    piece, back_img, back_far, back_near = lax.optimization_barrier(
        (piece, back_img, back_far, back_near)
    )
    du_img = backward(got["z_img"], got["inv_img"], own, back_img)
    du_txt = backward(got["z_txt"], got["inv_txt"], got["dz_txt"], back_near, back_far)
    image_grads = feature_grads(du_img, image_head)
    text_grads = feature_grads(du_txt, text_head)

    piece = join_z(swap(sum_spread(piece), "z"), lax.axis_size(("xh", "y")))
    parts = lax.axis_size(("xh", "z", "y")) * lax.axis_size(("xl", "c"))
    head_grads = finish(1.0 / parts, swap(piece, ("xh", "y")))
    return (image_grads, text_grads, head_grads)


def solution(mesh):
    fine = Mesh(mesh.devices.reshape(2, 8, 4, 2, 2), ROWS)
    split = P(ROWS, None)
    return jax.shard_map(
        per_device,
        mesh=fine,
        in_specs=(split, split, P(), P(), P(), P()),
        out_specs=(split, split, P(("xl", "c"), None)),
        check_vma=False,
    )
```

```python
import functools

import jax
import jax.numpy as jnp
from jax import lax
from jax.experimental import pallas as pl
from jax.experimental.pallas import tpu as pltpu
from jax.sharding import Mesh, PartitionSpec as P

ROWS = ("xh", "z", "y", "xl", "c")
X_RING = ("xh", "xl")
SWAP = [(0, 1), (1, 0)]
CROSS = [(0, 3), (3, 0), (1, 2), (2, 1)]
F32 = jnp.float32
BF16 = jnp.bfloat16
LANES_BOTH = (((1,), (1,)), ((), ()))
ROWS_BOTH = (((0,), (0,)), ((), ()))


def shape(dims, dtype):
    return jax.ShapeDtypeStruct(dims, dtype)


def local(kernel, outs, *args, scalars=0, scratch=(), mib=16):
    vmem = pl.BlockSpec(memory_space=pltpu.VMEM)
    smem = pl.BlockSpec(memory_space=pltpu.SMEM)
    many = isinstance(outs, (tuple, list))
    return pl.pallas_call(
        kernel,
        out_shape=outs,
        in_specs=[smem] * scalars + [vmem] * (len(args) - scalars),
        out_specs=[vmem] * len(outs) if many else vmem,
        scratch_shapes=scratch,
        compiler_params=pltpu.CompilerParams(vmem_limit_bytes=mib << 20),
        cost_estimate=pl.CostEstimate(flops=1000, bytes_accessed=1000, transcendentals=0),
    )(*args)


def embedding(feats, head):
    u = jnp.dot(feats, head, preferred_element_type=F32)
    inv = lax.rsqrt(jnp.sum(u * u, axis=1, keepdims=True) + 1e-06)
    return u * inv, inv


def tangent(z, inv, dz):
    return inv * (dz - z * jnp.sum(z * dz, axis=1, keepdims=True))


def over_rows(a, b):
    return lax.dot_general(a, b, ROWS_BOTH, preferred_element_type=F32)


def embed_kernel(head_ref, feats_ref, zb_ref, late_ref, inv_ref):
    z, inv = embedding(feats_ref[...], head_ref[...])
    zb_ref[...] = z.astype(BF16)
    late_ref[...] = z.astype(BF16)
    inv_ref[...] = inv


def embed(head, feats):
    rows, wide = feats.shape
    block = shape((rows, wide), BF16)
    return local(embed_kernel, [block, block, shape((rows, 1), F32)], head, feats)


def embed_other_kernel(head_ref, feats_ref, zb_ref):
    zb_ref[...] = embedding(feats_ref[...], head_ref[...])[0].astype(BF16)


def embed_other(head, feats):
    return local(embed_other_kernel, shape(feats.shape, BF16), head, feats)


def weigh(scale, bias, txt, img_refs, w_ref, home):
    weights = []
    for i, img_ref in enumerate(img_refs):
        logits = (
            scale * lax.dot_general(txt, img_ref[...], LANES_BOTH, preferred_element_type=F32)
            + bias
        )
        if home and i == 0:
            row_ids = lax.broadcasted_iota(jnp.int32, logits.shape, 0)
            col_ids = lax.broadcasted_iota(jnp.int32, logits.shape, 1)
            sign = jnp.where(row_ids == col_ids, 1.0, -1.0).astype(F32)
            deriv = -sign * jax.nn.sigmoid(-sign * logits)
        else:
            deriv = jax.nn.sigmoid(logits)
        weights.append((scale * deriv).astype(BF16))
        w_ref[i] = weights[-1]
    return weights


def gather(weights, img_refs):
    total = None
    for w, img_ref in zip(weights, img_refs):
        part = jnp.dot(w, img_ref[...], preferred_element_type=F32)
        total = part if total is None else total + part
    return total


def home_first_kernel(scale_ref, bias_ref, feats_ref, head_ref, *refs):
    img_refs, (zb_ref, inv_ref, w_ref) = refs[:-3], refs[-3:]
    z, inv = embedding(feats_ref[...], head_ref[...])
    txt = z.astype(BF16)
    zb_ref[...] = txt
    inv_ref[...] = inv
    weigh(scale_ref[0], bias_ref[0], txt, img_refs, w_ref, True)


def home_first(scale, bias, feats, head, imgs):
    rows, wide = feats.shape
    outs = [
        shape((rows, wide), BF16),
        shape((rows, 1), F32),
        shape((len(imgs), rows, imgs[0].shape[0]), BF16),
    ]
    return local(home_first_kernel, outs, scale, bias, feats, head, *imgs, scalars=2)


def group_kernel(scale_ref, bias_ref, zb_ref, inv_ref, first_ref, feats_ref, head_ref, *refs):
    img_refs, (w_ref, dz_ref, du_ref), near_refs = refs[:4], refs[4:7], refs[7:]
    txt = zb_ref[...]
    done = first_ref.shape[0]
    weights = weigh(scale_ref[0], bias_ref[0], txt, img_refs[done:], w_ref, False)
    dz = gather([first_ref[i] for i in range(done)] + weights, img_refs)
    dz_ref[...] = dz.astype(BF16)
    du_ref[...] = tangent(txt.astype(F32), inv_ref[...], dz).astype(BF16)
    text_kernel(scale_ref, bias_ref, feats_ref, head_ref, *img_refs, *near_refs)


def group_block(scale, bias, zb, inv, first, feats, head, imgs):
    rows, wide = zb.shape
    block = shape((rows, wide), BF16)
    outs = [shape((len(imgs) - first.shape[0],) + first.shape[1:], BF16), block, block]
    outs += [block, shape((len(imgs),) + first.shape[1:], BF16), block, block]
    return local(group_kernel, outs, scale, bias, zb, inv, first, feats, head, *imgs, scalars=2)


def text_kernel(scale_ref, bias_ref, feats_ref, head_ref, *refs):
    img_refs, (zb_ref, w_ref, dz_ref, du_ref) = refs[:-4], refs[-4:]
    z, inv = embedding(feats_ref[...], head_ref[...])
    txt = z.astype(BF16)
    zb_ref[...] = txt
    dz = gather(weigh(scale_ref[0], bias_ref[0], txt, img_refs, w_ref, False), img_refs)
    dz_ref[...] = dz.astype(BF16)
    du_ref[...] = tangent(z, inv, dz).astype(BF16)


def text_block(scale, bias, feats, head, imgs):
    rows, wide = feats.shape
    block = shape((rows, wide), BF16)
    outs = [block, shape((len(imgs), rows, imgs[0].shape[0]), BF16), block, block]
    return local(text_kernel, outs, scale, bias, feats, head, *imgs, scalars=2)


def part_by_core(core, acc_ref, keep_ref, send_ref):
    rows = keep_ref.shape[1]
    for k in range(2):
        mine = pl.multiple_of((2 * k + core) * rows, 8)
        other = pl.multiple_of((2 * k + 1 - core) * rows, 8)
        send_ref[k] = acc_ref[pl.ds(other, rows), :].astype(BF16)
        keep_ref[k] = acc_ref[pl.ds(mine, rows), :].astype(BF16)


def text_head_kernel(core_ref, *refs):
    pairs, (keep_ref, send_ref, acc_ref) = refs[:-3], refs[-3:]
    total = None
    for i in range(0, len(pairs), 2):
        part = over_rows(pairs[i][...], pairs[i + 1][...])
        total = part if total is None else total + part
    acc_ref[...] = total
    part_by_core(core_ref[0], acc_ref, keep_ref, send_ref)


def text_head_part(core, *pairs):
    depth, wide = pairs[0].shape[1], pairs[1].shape[1]
    half = shape((2, depth // 4, wide), BF16)
    return local(
        text_head_kernel,
        [half, half],
        core,
        *pairs,
        scalars=1,
        scratch=[pltpu.VMEM((depth, wide), F32)],
        mib=20,
    )


def image_side_kernel(count, *refs):
    txt_refs, w_refs, first_ref, rest_ref = (
        refs[:count],
        refs[count : 2 * count - 1],
        refs[2 * count - 1],
        refs[2 * count],
    )
    keep_ref, send_ref = refs[-2:]
    for i in (1, 3, 0, 2):
        weights = [first_ref[i] if i < 2 else rest_ref[i - 2]] + [ref[i] for ref in w_refs]
        dz = None
        for w, txt_ref in zip(weights, txt_refs):
            part = over_rows(w, txt_ref[...])
            dz = part if dz is None else dz + part
        if i % 2 == 0:
            keep_ref[i // 2] = dz
        else:
            send_ref[i // 2] = dz.astype(BF16)


def image_side(txts, weights, home):
    rows, wide = txts[0].shape
    dims = (2, rows, wide)
    return local(
        functools.partial(image_side_kernel, len(txts)),
        [shape(dims, F32), shape(dims, BF16)],
        *txts,
        *weights,
        *home,
        mib=20,
    )


def image_head_kernel(core_ref, keep_ref, got_ref, *refs):
    zb_refs, inv_refs, feats_refs = refs[:2], refs[2:4], refs[4:6]
    own_ref, next_ref, left_ref, send_ref, acc_ref = refs[6:]
    total = None
    for i in (1, 0):
        dz = keep_ref[i] + got_ref[i].astype(F32)
        if i == 0:
            own_ref[...] = dz.astype(BF16)
        else:
            next_ref[...] = dz.astype(BF16)
        du = tangent(zb_refs[i][...].astype(F32), inv_refs[i][...], dz).astype(BF16)
        part = over_rows(feats_refs[i][...], du)
        total = part if total is None else total + part
    acc_ref[...] = total
    part_by_core(core_ref[0], acc_ref, left_ref, send_ref)


def image_head_part(core, keep, got, zbs, invs, feats):
    dims = keep.shape[1:]
    block = shape(dims, BF16)
    depth = feats[0].shape[1]
    half = shape((2, depth // 4, dims[1]), BF16)
    return local(
        image_head_kernel,
        [block, block, half, half],
        core,
        keep,
        got,
        *zbs,
        *invs,
        *feats,
        scalars=1,
        scratch=[pltpu.VMEM((depth, dims[1]), F32)],
        mib=24,
    )


def split_x_kernel(got_ref, keep_ref, out_ref):
    rows = out_ref.shape[1]
    for k in range(out_ref.shape[0]):
        at = pl.ds(k % 2 * rows, rows)
        out_ref[k] = (keep_ref[k // 2, at].astype(F32) + got_ref[k // 2, at].astype(F32)).astype(BF16)


def split_x(keep, got):
    _, rows, wide = keep.shape
    return local(split_x_kernel, shape((4, rows // 2, wide), BF16), got, keep)


def split_y_kernel(me_ref, got_ref, keep_ref, *refs):
    outs, held = refs[:-1], refs[-1]
    count, blocks, rows, _ = held.shape
    total = (keep_ref[...].astype(F32) + got_ref[...].astype(F32)).astype(BF16)
    for b in range(blocks):
        for k in range(count):
            at = (b % 2 * count + k) * rows
            held[k, b] = total[b // 2, at : at + rows]
    for s, out_ref in enumerate(outs):
        out_ref[...] = held[lax.rem(me_ref[0] + s, count)]


def split_y(me, keep, got):
    count = lax.axis_size("y")
    _, rows, wide = keep.shape
    part = (4, rows // 2 // count, wide)
    return local(
        split_y_kernel,
        [shape(part, BF16)] * count,
        me,
        got,
        keep,
        scalars=1,
        scratch=[pltpu.VMEM((count,) + part, BF16)],
    )


def sum_of(ref):
    total = ref[0].astype(F32)
    for k in range(1, ref.shape[0]):
        total = total + ref[k].astype(F32)
    return total


def sum_kernel(*refs):
    total = refs[0][...].astype(F32)
    for ref in refs[1:-1]:
        total = total + ref[...].astype(F32)
    refs[-1][...] = total.astype(BF16)


def add_up(*parts):
    return local(sum_kernel, shape(parts[0].shape, BF16), *parts)


def sum_split_y_kernel(me_ref, in_ref, *refs):
    outs, held = refs[:-1], refs[-1]
    total = sum_of(in_ref).astype(BF16)
    count, rows, _ = held.shape
    for k in range(count):
        held[k] = total[k * rows : (k + 1) * rows]
    for s, out_ref in enumerate(outs):
        out_ref[...] = held[lax.rem(me_ref[0] + s, count)]


def sum_split_y(me, parts):
    count = lax.axis_size("y")
    _, rows, wide = parts.shape
    part = (rows // count, wide)
    return local(
        sum_split_y_kernel,
        [shape(part, BF16)] * count,
        me,
        parts,
        scalars=1,
        scratch=[pltpu.VMEM((count,) + part, BF16)],
    )


def split_z_kernel(img_ref, *refs):
    txt_refs, out_ref = refs[:-1], refs[-1]
    txt = txt_refs[0][...].astype(F32)
    for ref in txt_refs[1:]:
        txt = txt + ref[...].astype(F32)
    both = jnp.concatenate([sum_of(img_ref), txt], axis=0).astype(BF16)
    rows = out_ref.shape[1]
    for k in range(out_ref.shape[0]):
        out_ref[k] = both[k * rows : (k + 1) * rows]


def split_z(img, txts):
    count = lax.axis_size("z")
    _, rows, wide = img.shape
    return local(split_z_kernel, shape((count, 2 * rows // count, wide), BF16), img, *txts)


def sum_spread_kernel(in_ref, out_ref):
    total = sum_of(in_ref).astype(BF16)
    for k in range(out_ref.shape[0]):
        out_ref[k] = total


def sum_spread(parts):
    return local(sum_spread_kernel, shape(parts.shape, BF16), parts)


def join_z_kernel(in_ref, out_ref):
    both = jnp.concatenate([in_ref[k] for k in range(in_ref.shape[0])], axis=0)
    for k in range(out_ref.shape[0]):
        out_ref[k] = both


def join_z(pieces, copies):
    count, rows, wide = pieces.shape
    return local(join_z_kernel, shape((copies, count * rows, wide), BF16), pieces)


def finish_kernel(part, in_ref, out_ref):
    count, both, wide = in_ref.shape
    rows = both // 2
    for k in range(count):
        for j in range(2):
            out_ref[k * rows : (k + 1) * rows, j * wide : (j + 1) * wide] = (
                in_ref[k, j * rows : (j + 1) * rows].astype(F32) * part
            )


def finish(part, pieces):
    count, both, wide = pieces.shape
    return local(
        functools.partial(finish_kernel, part), shape((count * both // 2, 2 * wide), F32), pieces
    )


def grads_kernel(feats_ref, head_ref, *refs):
    parts, out_ref = refs[:-1], refs[-1]
    z, inv = embedding(feats_ref[...], head_ref[...])
    dz = parts[0][...].astype(F32)
    for ref in parts[1:]:
        dz = dz + ref[...].astype(F32)
    du = tangent(z, inv, dz).astype(BF16)
    out = lax.dot_general(du, head_ref[...], LANES_BOTH, preferred_element_type=F32)
    out_ref[...] = out.astype(BF16)


def feature_grads(feats, head, *parts):
    return local(grads_kernel, shape(feats.shape, BF16), feats, head, *parts)


def far_z(block):
    count = lax.axis_size("z")
    return lax.ppermute(block, "z", [(i, (i + count // 2) % count) for i in range(count)])


def along_y(parts):
    count = lax.axis_size("y")
    return [parts[0]] + [
        lax.ppermute(part, "y", [(i, (i + s) % count) for i in range(count)])
        for s, part in enumerate(parts)
        if s > 0
    ]


def swap(block, axes):
    return lax.all_to_all(block, axes, 0, 0, tiled=True)


def per_device(image_feats, text_feats, image_head, text_head, scale, bias):
    core = lax.axis_index("c").astype(jnp.int32).reshape(1)
    me_y = lax.axis_index("y").astype(jnp.int32).reshape(1)

    def unit(work):
        def nothing():
            return jax.tree.map(lambda s: jnp.zeros(s.shape, s.dtype), jax.eval_shape(work))

        return lax.cond(scale[0] > 0, work, nothing)

    far = far_z(text_feats)

    near = lax.ppermute(text_feats, X_RING, CROSS)
    next_feats = lax.ppermute(image_feats, "xl", SWAP)

    def own_unit():
        core_feats = lax.ppermute(image_feats, "c", SWAP)
        zb_img, late_img, inv_img = embed(image_head, image_feats)
        zb_core = embed_other(image_head, core_feats)
        zb_txt, inv_txt, w_first = home_first(
            scale, bias, text_feats, text_head, [zb_img, zb_core]
        )
        return zb_img, zb_core, late_img, inv_img, zb_txt, inv_txt, w_first

    zb_img, zb_core, late_img, inv_img, zb_txt, inv_txt, w_first = unit(own_unit)
    near, next_feats, w_first = lax.optimization_barrier((near, next_feats, w_first))

    def group_unit():
        next_core_feats = lax.ppermute(next_feats, "c", SWAP)
        zb_next, late_next, inv_next = embed(image_head, next_feats)
        zb_next_core = embed_other(image_head, next_core_feats)
        imgs = [zb_img, zb_core, zb_next, zb_next_core]
        w_rest, dz_txt, du_home, zb_near, w_near, back_near, du_near = group_block(
            scale, bias, zb_txt, inv_txt, w_first, near, text_head, imgs
        )
        return dict(
            imgs=imgs[2:],
            late=late_next,
            inv=inv_next,
            w_rest=w_rest,
            dz_txt=dz_txt,
            zb_near=zb_near,
            w_near=w_near,
            back_near=back_near,
            dus=[du_home, du_near],
        )

    got = unit(group_unit)
    far, dus = lax.optimization_barrier((far, got["dus"]))
    zb_far, w_far, back_far, du_far = text_block(
        scale, bias, far, text_head, [zb_img, zb_core] + got["imgs"]
    )
    back_far = far_z(back_far)
    back_near = lax.ppermute(got["back_near"], X_RING, CROSS)
    keep_dz, send_dz = image_side(
        [zb_txt, got["zb_near"], zb_far], [got["w_near"], w_far], [w_first, got["w_rest"]]
    )
    got_dz = lax.ppermute(send_dz, "c", SWAP)
    keep_dz, du_far = lax.optimization_barrier((keep_dz, du_far))
    keep_txt, send = text_head_part(core, far, du_far, text_feats, dus[0], near, dus[1])
    got_txt = lax.ppermute(send, "c", SWAP)
    keep_txt, got_dz = lax.optimization_barrier((keep_txt, got_dz))
    own, send, keep, part = image_head_part(
        core, keep_dz, got_dz, [late_img, got["late"]], [inv_img, got["inv"]], [image_feats, next_feats]
    )
    got_img = lax.ppermute(part, "c", SWAP)
    txt = split_x(keep_txt, got_txt)
    txt, got_img = lax.optimization_barrier((txt, got_img))
    txt = swap(txt, ("xl", "xh"))
    img = along_y(split_y(me_y, keep, got_img))
    txt, img = lax.optimization_barrier((sum_split_y(me_y, txt), img))
    img = add_up(*img)

    def second_unit():
        return split_z(swap(img, ("xl", "xh")), along_y(txt))

    piece, send = lax.optimization_barrier((unit(second_unit), send))
    back_img = lax.ppermute(send, "xl", SWAP)
    piece, back_far, back_near = lax.optimization_barrier((piece, back_far, back_near))
    piece = swap(piece, "z")
    piece, back_img, back_far, back_near = lax.optimization_barrier(
        (piece, back_img, back_far, back_near)
    )
    image_grads = feature_grads(image_feats, image_head, own, back_img)
    text_grads = feature_grads(text_feats, text_head, got["dz_txt"], back_near, back_far)

    piece = join_z(swap(sum_spread(piece), "z"), lax.axis_size(("xh", "y")))
    parts = lax.axis_size(("xh", "z", "y")) * lax.axis_size(("xl", "c"))
    head_grads = finish(1.0 / parts, swap(piece, ("xh", "y")))
    return (image_grads, text_grads, head_grads)


def solution(mesh):
    fine = Mesh(mesh.devices.reshape(2, 8, 4, 2, 2), ROWS)
    split = P(ROWS, None)
    return jax.shard_map(
        per_device,
        mesh=fine,
        in_specs=(split, split, P(), P(), P(), P()),
        out_specs=(split, split, P(("xl", "c"), None)),
        check_vma=False,
    )
```

```python
import functools

import jax
import jax.numpy as jnp
from jax import lax
from jax.experimental import pallas as pl
from jax.experimental.pallas import tpu as pltpu
from jax.sharding import Mesh, PartitionSpec as P

ROWS = ("xh", "z", "y", "xl", "c")
X_RING = ("xh", "xl")
SWAP = [(0, 1), (1, 0)]
CROSS = [(0, 3), (3, 0), (1, 2), (2, 1)]
F32 = jnp.float32
BF16 = jnp.bfloat16
LANES_BOTH = (((1,), (1,)), ((), ()))
ROWS_BOTH = (((0,), (0,)), ((), ()))


def shape(dims, dtype):
    return jax.ShapeDtypeStruct(dims, dtype)


def local(kernel, outs, *args, scalars=0, scratch=(), mib=16):
    vmem = pl.BlockSpec(memory_space=pltpu.VMEM)
    smem = pl.BlockSpec(memory_space=pltpu.SMEM)
    many = isinstance(outs, (tuple, list))
    return pl.pallas_call(
        kernel,
        out_shape=outs,
        in_specs=[smem] * scalars + [vmem] * (len(args) - scalars),
        out_specs=[vmem] * len(outs) if many else vmem,
        scratch_shapes=scratch,
        compiler_params=pltpu.CompilerParams(vmem_limit_bytes=mib << 20),
        cost_estimate=pl.CostEstimate(flops=1000, bytes_accessed=1000, transcendentals=0),
    )(*args)


def embedding(feats, head):
    u = jnp.dot(feats, head, preferred_element_type=F32)
    inv = lax.rsqrt(jnp.sum(u * u, axis=1, keepdims=True) + 1e-06)
    return u * inv, inv


def tangent(z, inv, dz):
    return inv * (dz - z * jnp.sum(z * dz, axis=1, keepdims=True))


def over_rows(a, b):
    return lax.dot_general(a, b, ROWS_BOTH, preferred_element_type=F32)


def embed_kernel(head_ref, feats_ref, zb_ref, late_ref, inv_ref):
    z, inv = embedding(feats_ref[...], head_ref[...])
    zb_ref[...] = z.astype(BF16)
    late_ref[...] = z.astype(BF16)
    inv_ref[...] = inv


def embed(head, feats):
    rows, wide = feats.shape
    block = shape((rows, wide), BF16)
    return local(embed_kernel, [block, block, shape((rows, 1), F32)], head, feats)


def embed_other_kernel(head_ref, feats_ref, zb_ref):
    zb_ref[...] = embedding(feats_ref[...], head_ref[...])[0].astype(BF16)


def embed_other(head, feats):
    return local(embed_other_kernel, shape(feats.shape, BF16), head, feats)


def weigh(scale, bias, txt, img_refs, w_ref, home):
    weights = []
    for i, img_ref in enumerate(img_refs):
        logits = (
            scale * lax.dot_general(txt, img_ref[...], LANES_BOTH, preferred_element_type=F32)
            + bias
        )
        if home and i == 0:
            row_ids = lax.broadcasted_iota(jnp.int32, logits.shape, 0)
            col_ids = lax.broadcasted_iota(jnp.int32, logits.shape, 1)
            sign = jnp.where(row_ids == col_ids, 1.0, -1.0).astype(F32)
            deriv = -sign * jax.nn.sigmoid(-sign * logits)
        else:
            deriv = jax.nn.sigmoid(logits)
        weights.append((scale * deriv).astype(BF16))
        w_ref[i] = weights[-1]
    return weights


def gather(weights, img_refs):
    total = None
    for w, img_ref in zip(weights, img_refs):
        part = jnp.dot(w, img_ref[...], preferred_element_type=F32)
        total = part if total is None else total + part
    return total


def home_first_kernel(scale_ref, bias_ref, feats_ref, head_ref, *refs):
    img_refs, (zb_ref, inv_ref, w_ref) = refs[:-3], refs[-3:]
    z, inv = embedding(feats_ref[...], head_ref[...])
    txt = z.astype(BF16)
    zb_ref[...] = txt
    inv_ref[...] = inv
    weigh(scale_ref[0], bias_ref[0], txt, img_refs, w_ref, True)


def home_first(scale, bias, feats, head, imgs):
    rows, wide = feats.shape
    outs = [
        shape((rows, wide), BF16),
        shape((rows, 1), F32),
        shape((len(imgs), rows, imgs[0].shape[0]), BF16),
    ]
    return local(home_first_kernel, outs, scale, bias, feats, head, *imgs, scalars=2)


def group_kernel(scale_ref, bias_ref, zb_ref, inv_ref, first_ref, feats_ref, head_ref, *refs):
    img_refs, (w_ref, dz_ref, du_ref), near_refs = refs[:4], refs[4:7], refs[7:]
    txt = zb_ref[...]
    done = first_ref.shape[0]
    weights = weigh(scale_ref[0], bias_ref[0], txt, img_refs[done:], w_ref, False)
    dz = gather([first_ref[i] for i in range(done)] + weights, img_refs)
    dz_ref[...] = dz.astype(BF16)
    du_ref[...] = tangent(txt.astype(F32), inv_ref[...], dz).astype(BF16)
    text_kernel(scale_ref, bias_ref, feats_ref, head_ref, *img_refs, *near_refs)


def group_block(scale, bias, zb, inv, first, feats, head, imgs):
    rows, wide = zb.shape
    block = shape((rows, wide), BF16)
    outs = [shape((len(imgs) - first.shape[0],) + first.shape[1:], BF16), block, block]
    outs += [block, shape((len(imgs),) + first.shape[1:], BF16), block, block]
    return local(group_kernel, outs, scale, bias, zb, inv, first, feats, head, *imgs, scalars=2)


def text_kernel(scale_ref, bias_ref, feats_ref, head_ref, *refs):
    img_refs, (zb_ref, w_ref, dz_ref, du_ref) = refs[:-4], refs[-4:]
    z, inv = embedding(feats_ref[...], head_ref[...])
    txt = z.astype(BF16)
    zb_ref[...] = txt
    dz = gather(weigh(scale_ref[0], bias_ref[0], txt, img_refs, w_ref, False), img_refs)
    dz_ref[...] = dz.astype(BF16)
    du_ref[...] = tangent(z, inv, dz).astype(BF16)


def text_block(scale, bias, feats, head, imgs):
    rows, wide = feats.shape
    block = shape((rows, wide), BF16)
    outs = [block, shape((len(imgs), rows, imgs[0].shape[0]), BF16), block, block]
    return local(text_kernel, outs, scale, bias, feats, head, *imgs, scalars=2)


def part_by_core(core, acc_ref, keep_ref, send_ref):
    rows = keep_ref.shape[1]
    for k in range(2):
        mine = pl.multiple_of((2 * k + core) * rows, 8)
        other = pl.multiple_of((2 * k + 1 - core) * rows, 8)
        send_ref[k] = acc_ref[pl.ds(other, rows), :].astype(BF16)
        keep_ref[k] = acc_ref[pl.ds(mine, rows), :].astype(BF16)


def text_head_kernel(core_ref, *refs):
    pairs, (keep_ref, send_ref, acc_ref) = refs[:-3], refs[-3:]
    total = None
    for i in range(0, len(pairs), 2):
        part = over_rows(pairs[i][...], pairs[i + 1][...])
        total = part if total is None else total + part
    acc_ref[...] = total
    part_by_core(core_ref[0], acc_ref, keep_ref, send_ref)


def text_head_part(core, *pairs):
    depth, wide = pairs[0].shape[1], pairs[1].shape[1]
    half = shape((2, depth // 4, wide), BF16)
    return local(
        text_head_kernel,
        [half, half],
        core,
        *pairs,
        scalars=1,
        scratch=[pltpu.VMEM((depth, wide), F32)],
        mib=20,
    )


def image_side_kernel(count, *refs):
    txt_refs, w_refs, first_ref, rest_ref = (
        refs[:count],
        refs[count : 2 * count - 1],
        refs[2 * count - 1],
        refs[2 * count],
    )
    keep_ref, send_ref = refs[-2:]
    for i in (1, 3, 0, 2):
        weights = [first_ref[i] if i < 2 else rest_ref[i - 2]] + [ref[i] for ref in w_refs]
        dz = None
        for w, txt_ref in zip(weights, txt_refs):
            part = over_rows(w, txt_ref[...])
            dz = part if dz is None else dz + part
        if i % 2 == 0:
            keep_ref[i // 2] = dz
        else:
            send_ref[i // 2] = dz.astype(BF16)


def image_side(txts, weights, home):
    rows, wide = txts[0].shape
    dims = (2, rows, wide)
    return local(
        functools.partial(image_side_kernel, len(txts)),
        [shape(dims, F32), shape(dims, BF16)],
        *txts,
        *weights,
        *home,
        mib=20,
    )


def image_head_kernel(core_ref, keep_ref, got_ref, *refs):
    zb_refs, inv_refs, feats_refs = refs[:2], refs[2:4], refs[4:6]
    own_ref, next_ref, left_ref, send_ref, acc_ref = refs[6:]
    total = None
    for i in (1, 0):
        dz = keep_ref[i] + got_ref[i].astype(F32)
        if i == 0:
            own_ref[...] = dz.astype(BF16)
        else:
            next_ref[...] = dz.astype(BF16)
        du = tangent(zb_refs[i][...].astype(F32), inv_refs[i][...], dz).astype(BF16)
        part = over_rows(feats_refs[i][...], du)
        total = part if total is None else total + part
    acc_ref[...] = total
    part_by_core(core_ref[0], acc_ref, left_ref, send_ref)


def image_head_part(core, keep, got, zbs, invs, feats):
    dims = keep.shape[1:]
    block = shape(dims, BF16)
    depth = feats[0].shape[1]
    half = shape((2, depth // 4, dims[1]), BF16)
    return local(
        image_head_kernel,
        [block, block, half, half],
        core,
        keep,
        got,
        *zbs,
        *invs,
        *feats,
        scalars=1,
        scratch=[pltpu.VMEM((depth, dims[1]), F32)],
        mib=24,
    )


def split_x_kernel(got_ref, keep_ref, out_ref):
    rows = out_ref.shape[1]
    for k in range(out_ref.shape[0]):
        at = pl.ds(k % 2 * rows, rows)
        out_ref[k] = (keep_ref[k // 2, at].astype(F32) + got_ref[k // 2, at].astype(F32)).astype(BF16)


def split_x(keep, got):
    _, rows, wide = keep.shape
    return local(split_x_kernel, shape((4, rows // 2, wide), BF16), got, keep)


def split_y_kernel(me_ref, got_ref, keep_ref, *refs):
    outs, held = refs[:-1], refs[-1]
    count, tall, _ = held.shape
    rows = tall // 4
    total = keep_ref[...].astype(F32) + got_ref[...].astype(F32)
    for k in range(count):
        at = [(b // 2, (b % 2 * count + k) * rows) for b in range(4)]
        held[k] = jnp.concatenate([total[h, r : r + rows] for h, r in at], axis=0).astype(BF16)
    for s, out_ref in enumerate(outs):
        out_ref[...] = held[lax.rem(me_ref[0] + s, count)]


def split_y(me, keep, got):
    count = lax.axis_size("y")
    _, rows, wide = keep.shape
    part = (2 * rows // count, wide)
    return local(
        split_y_kernel,
        [shape(part, BF16)] * count,
        me,
        got,
        keep,
        scalars=1,
        scratch=[pltpu.VMEM((count,) + part, BF16)],
    )


def sum_of(ref):
    total = ref[0].astype(F32)
    for k in range(1, ref.shape[0]):
        total = total + ref[k].astype(F32)
    return total


def sum_kernel(*refs):
    total = refs[0][...].astype(F32)
    for ref in refs[1:-1]:
        total = total + ref[...].astype(F32)
    out_ref = refs[-1]
    rows = out_ref.shape[1]
    for k in range(out_ref.shape[0]):
        out_ref[k] = total[k * rows : (k + 1) * rows].astype(BF16)


def add_up(*parts):
    rows, wide = parts[0].shape
    return local(sum_kernel, shape((4, rows // 4, wide), BF16), *parts)


def sum_split_y_kernel(in_ref, out_ref):
    total = sum_of(in_ref).astype(BF16)
    rows = out_ref.shape[1]
    for k in range(out_ref.shape[0]):
        out_ref[k] = total[k * rows : (k + 1) * rows]


def sum_split_y(parts):
    count = lax.axis_size("y")
    _, rows, wide = parts.shape
    return local(sum_split_y_kernel, shape((count, rows // count, wide), BF16), parts)


def split_z_kernel(img_ref, txt_ref, out_ref):
    both = jnp.concatenate([sum_of(img_ref), sum_of(txt_ref)], axis=0)
    cols = [both[:, at : at + 128] for at in range(0, both.shape[1], 128)]
    tall = jnp.concatenate(cols, axis=0)
    rows = out_ref.shape[1]
    for k in range(out_ref.shape[0]):
        out_ref[k] = tall[k * rows : (k + 1) * rows].astype(BF16)


def split_z(img, txt):
    count = lax.axis_size("z")
    _, rows, wide = img.shape
    dims = (count, 2 * rows * wide // 128 // count, 128)
    return local(split_z_kernel, shape(dims, BF16), img, txt)


def sum_spread_kernel(in_ref, out_ref):
    total = sum_of(in_ref).astype(BF16)
    for k in range(out_ref.shape[0]):
        out_ref[k] = total


def sum_spread(parts):
    return local(sum_spread_kernel, shape(parts.shape, BF16), parts)


def join_z_kernel(in_ref, out_ref):
    tall = jnp.concatenate([in_ref[k].astype(F32) for k in range(in_ref.shape[0])], axis=0)
    rows, wide = out_ref.shape[1:]
    cols = [tall[k * rows : (k + 1) * rows] for k in range(wide // 128)]
    both = jnp.concatenate(cols, axis=1).astype(BF16)
    for k in range(out_ref.shape[0]):
        out_ref[k] = both


def join_z(pieces, wide, copies):
    count, rows, lanes = pieces.shape
    return local(join_z_kernel, shape((copies, count * rows * lanes // wide, wide), BF16), pieces)


def finish_kernel(part, in_ref, out_ref):
    count, both, wide = in_ref.shape
    rows = both // 2
    for k in range(count):
        for j in range(2):
            out_ref[k * rows : (k + 1) * rows, j * wide : (j + 1) * wide] = (
                in_ref[k, j * rows : (j + 1) * rows].astype(F32) * part
            )


def finish(part, pieces):
    count, both, wide = pieces.shape
    return local(
        functools.partial(finish_kernel, part), shape((count * both // 2, 2 * wide), F32), pieces
    )


def grads_kernel(feats_ref, head_ref, *refs):
    parts, out_ref = refs[:-1], refs[-1]
    z, inv = embedding(feats_ref[...], head_ref[...])
    dz = parts[0][...].astype(F32)
    for ref in parts[1:]:
        dz = dz + ref[...].astype(F32)
    du = tangent(z, inv, dz).astype(BF16)
    out = lax.dot_general(du, head_ref[...], LANES_BOTH, preferred_element_type=F32)
    out_ref[...] = out.astype(BF16)


def feature_grads(feats, head, *parts):
    return local(grads_kernel, shape(feats.shape, BF16), feats, head, *parts)


def far_z(block):
    count = lax.axis_size("z")
    return lax.ppermute(block, "z", [(i, (i + count // 2) % count) for i in range(count)])


def along_y(parts):
    count = lax.axis_size("y")
    return [parts[0]] + [
        lax.ppermute(part, "y", [(i, (i + s) % count) for i in range(count)])
        for s, part in enumerate(parts)
        if s > 0
    ]


def swap(block, axes):
    return lax.all_to_all(block, axes, 0, 0, tiled=True)


def per_device(image_feats, text_feats, image_head, text_head, scale, bias):
    core = lax.axis_index("c").astype(jnp.int32).reshape(1)
    me_y = lax.axis_index("y").astype(jnp.int32).reshape(1)

    def unit(work):
        def nothing():
            return jax.tree.map(lambda s: jnp.zeros(s.shape, s.dtype), jax.eval_shape(work))

        return lax.cond(scale[0] > 0, work, nothing)

    far = far_z(text_feats)

    near = lax.ppermute(text_feats, X_RING, CROSS)
    next_feats = lax.ppermute(image_feats, "xl", SWAP)

    def own_unit():
        core_feats = lax.ppermute(image_feats, "c", SWAP)
        zb_img, late_img, inv_img = embed(image_head, image_feats)
        zb_core = embed_other(image_head, core_feats)
        zb_txt, inv_txt, w_first = home_first(
            scale, bias, text_feats, text_head, [zb_img, zb_core]
        )
        return zb_img, zb_core, late_img, inv_img, zb_txt, inv_txt, w_first

    zb_img, zb_core, late_img, inv_img, zb_txt, inv_txt, w_first = unit(own_unit)
    near, next_feats, w_first = lax.optimization_barrier((near, next_feats, w_first))

    def group_unit():
        next_core_feats = lax.ppermute(next_feats, "c", SWAP)
        zb_next, late_next, inv_next = embed(image_head, next_feats)
        zb_next_core = embed_other(image_head, next_core_feats)
        imgs = [zb_img, zb_core, zb_next, zb_next_core]
        w_rest, dz_txt, du_home, zb_near, w_near, back_near, du_near = group_block(
            scale, bias, zb_txt, inv_txt, w_first, near, text_head, imgs
        )
        return dict(
            imgs=imgs[2:],
            late=late_next,
            inv=inv_next,
            w_rest=w_rest,
            dz_txt=dz_txt,
            zb_near=zb_near,
            w_near=w_near,
            back_near=back_near,
            dus=[du_home, du_near],
        )

    got = unit(group_unit)
    far, dus = lax.optimization_barrier((far, got["dus"]))
    zb_far, w_far, back_far, du_far = text_block(
        scale, bias, far, text_head, [zb_img, zb_core] + got["imgs"]
    )
    back_far = far_z(back_far)
    back_near = lax.ppermute(got["back_near"], X_RING, CROSS)
    keep_dz, send_dz = image_side(
        [zb_txt, got["zb_near"], zb_far], [got["w_near"], w_far], [w_first, got["w_rest"]]
    )
    got_dz = lax.ppermute(send_dz, "c", SWAP)
    keep_dz, du_far = lax.optimization_barrier((keep_dz, du_far))
    keep_txt, send = text_head_part(core, far, du_far, text_feats, dus[0], near, dus[1])
    got_txt = lax.ppermute(send, "c", SWAP)
    keep_txt, got_dz = lax.optimization_barrier((keep_txt, got_dz))
    own, send, keep, part = image_head_part(
        core, keep_dz, got_dz, [late_img, got["late"]], [inv_img, got["inv"]], [image_feats, next_feats]
    )
    got_img = lax.ppermute(part, "c", SWAP)
    txt = split_x(keep_txt, got_txt)
    txt, got_img = lax.optimization_barrier((txt, got_img))
    txt = swap(txt, ("xl", "xh"))
    img = along_y(split_y(me_y, keep, got_img))
    txt = swap(sum_split_y(txt), "y")
    txt, img = lax.optimization_barrier((txt, add_up(*img)))

    def second_unit():
        return split_z(swap(img, ("xl", "xh")), txt)

    piece, send = lax.optimization_barrier((unit(second_unit), send))
    back_img = lax.ppermute(send, "xl", SWAP)
    piece, back_far, back_near = lax.optimization_barrier((piece, back_far, back_near))
    piece = swap(piece, "z")
    piece, back_img, back_far, back_near = lax.optimization_barrier(
        (piece, back_img, back_far, back_near)
    )
    image_grads = feature_grads(image_feats, image_head, own, back_img)
    text_grads = feature_grads(text_feats, text_head, got["dz_txt"], back_near, back_far)

    piece = join_z(swap(sum_spread(piece), "z"), image_head.shape[1], lax.axis_size(("xh", "y")))
    parts = lax.axis_size(("xh", "z", "y")) * lax.axis_size(("xl", "c"))
    head_grads = finish(1.0 / parts, swap(piece, ("xh", "y")))
    return (image_grads, text_grads, head_grads)


def solution(mesh):
    fine = Mesh(mesh.devices.reshape(2, 8, 4, 2, 2), ROWS)
    split = P(ROWS, None)
    return jax.shard_map(
        per_device,
        mesh=fine,
        in_specs=(split, split, P(), P(), P(), P()),
        out_specs=(split, split, P(("xl", "c"), None)),
        check_vma=False,
    )
```

```python
import functools

import jax
import jax.numpy as jnp
from jax import lax
from jax.experimental import pallas as pl
from jax.experimental.pallas import tpu as pltpu
from jax.sharding import Mesh, PartitionSpec as P

ROWS = ("xh", "z", "y", "xl", "c")
X_RING = ("xh", "xl")
SWAP = [(0, 1), (1, 0)]
CROSS = [(0, 3), (3, 0), (1, 2), (2, 1)]
F32 = jnp.float32
BF16 = jnp.bfloat16
LANES_BOTH = (((1,), (1,)), ((), ()))
ROWS_BOTH = (((0,), (0,)), ((), ()))


def shape(dims, dtype):
    return jax.ShapeDtypeStruct(dims, dtype)


def local(kernel, outs, *args, scalars=0, scratch=(), mib=16):
    vmem = pl.BlockSpec(memory_space=pltpu.VMEM)
    smem = pl.BlockSpec(memory_space=pltpu.SMEM)
    many = isinstance(outs, (tuple, list))
    return pl.pallas_call(
        kernel,
        out_shape=outs,
        in_specs=[smem] * scalars + [vmem] * (len(args) - scalars),
        out_specs=[vmem] * len(outs) if many else vmem,
        scratch_shapes=scratch,
        compiler_params=pltpu.CompilerParams(vmem_limit_bytes=mib << 20),
        cost_estimate=pl.CostEstimate(flops=1000, bytes_accessed=1000, transcendentals=0),
    )(*args)


def embedding(feats, head):
    u = jnp.dot(feats, head, preferred_element_type=F32)
    inv = lax.rsqrt(jnp.sum(u * u, axis=1, keepdims=True) + 1e-06)
    return u * inv, inv


def tangent(z, inv, dz):
    return inv * (dz - z * jnp.sum(z * dz, axis=1, keepdims=True))


def over_rows(a, b):
    return lax.dot_general(a, b, ROWS_BOTH, preferred_element_type=F32)


def embed_kernel(head_ref, feats_ref, zb_ref, late_ref, inv_ref):
    z, inv = embedding(feats_ref[...], head_ref[...])
    zb_ref[...] = z.astype(BF16)
    late_ref[...] = z.astype(BF16)
    inv_ref[...] = inv


def embed(head, feats):
    rows, wide = feats.shape
    block = shape((rows, wide), BF16)
    return local(embed_kernel, [block, block, shape((rows, 1), F32)], head, feats)


def embed_other_kernel(head_ref, feats_ref, zb_ref):
    zb_ref[...] = embedding(feats_ref[...], head_ref[...])[0].astype(BF16)


def embed_other(head, feats):
    return local(embed_other_kernel, shape(feats.shape, BF16), head, feats)


def weigh(scale, bias, txt, img_refs, w_ref, home):
    weights = []
    for i, img_ref in enumerate(img_refs):
        logits = (
            scale * lax.dot_general(txt, img_ref[...], LANES_BOTH, preferred_element_type=F32)
            + bias
        )
        if home and i == 0:
            row_ids = lax.broadcasted_iota(jnp.int32, logits.shape, 0)
            col_ids = lax.broadcasted_iota(jnp.int32, logits.shape, 1)
            sign = jnp.where(row_ids == col_ids, 1.0, -1.0).astype(F32)
            deriv = -sign * jax.nn.sigmoid(-sign * logits)
        else:
            deriv = jax.nn.sigmoid(logits)
        weights.append((scale * deriv).astype(BF16))
        w_ref[i] = weights[-1]
    return weights


def gather(weights, img_refs):
    total = None
    for w, img_ref in zip(weights, img_refs):
        part = jnp.dot(w, img_ref[...], preferred_element_type=F32)
        total = part if total is None else total + part
    return total


def home_first_kernel(scale_ref, bias_ref, feats_ref, head_ref, *refs):
    img_refs, (zb_ref, inv_ref, w_ref) = refs[:-3], refs[-3:]
    z, inv = embedding(feats_ref[...], head_ref[...])
    txt = z.astype(BF16)
    zb_ref[...] = txt
    inv_ref[...] = inv
    weigh(scale_ref[0], bias_ref[0], txt, img_refs, w_ref, True)


def home_first(scale, bias, feats, head, imgs):
    rows, wide = feats.shape
    outs = [
        shape((rows, wide), BF16),
        shape((rows, 1), F32),
        shape((len(imgs), rows, imgs[0].shape[0]), BF16),
    ]
    return local(home_first_kernel, outs, scale, bias, feats, head, *imgs, scalars=2)


def group_kernel(scale_ref, bias_ref, zb_ref, inv_ref, first_ref, feats_ref, head_ref, *refs):
    img_refs, (w_ref, dz_ref, du_ref), near_refs = refs[:4], refs[4:7], refs[7:]
    txt = zb_ref[...]
    done = first_ref.shape[0]
    weights = weigh(scale_ref[0], bias_ref[0], txt, img_refs[done:], w_ref, False)
    dz = gather([first_ref[i] for i in range(done)] + weights, img_refs)
    dz_ref[...] = dz.astype(BF16)
    du_ref[...] = tangent(txt.astype(F32), inv_ref[...], dz).astype(BF16)
    text_kernel(scale_ref, bias_ref, feats_ref, head_ref, *img_refs, *near_refs)


def group_block(scale, bias, zb, inv, first, feats, head, imgs):
    rows, wide = zb.shape
    block = shape((rows, wide), BF16)
    outs = [shape((len(imgs) - first.shape[0],) + first.shape[1:], BF16), block, block]
    outs += [block, shape((len(imgs),) + first.shape[1:], BF16), block, block]
    return local(group_kernel, outs, scale, bias, zb, inv, first, feats, head, *imgs, scalars=2)


def text_kernel(scale_ref, bias_ref, feats_ref, head_ref, *refs):
    img_refs, (zb_ref, w_ref, dz_ref, du_ref) = refs[:-4], refs[-4:]
    z, inv = embedding(feats_ref[...], head_ref[...])
    txt = z.astype(BF16)
    zb_ref[...] = txt
    dz = gather(weigh(scale_ref[0], bias_ref[0], txt, img_refs, w_ref, False), img_refs)
    dz_ref[...] = dz.astype(BF16)
    du_ref[...] = tangent(z, inv, dz).astype(BF16)


def text_block(scale, bias, feats, head, imgs):
    rows, wide = feats.shape
    block = shape((rows, wide), BF16)
    outs = [block, shape((len(imgs), rows, imgs[0].shape[0]), BF16), block, block]
    return local(text_kernel, outs, scale, bias, feats, head, *imgs, scalars=2)


def part_by_core(core, acc_ref, keep_ref, send_ref):
    rows = keep_ref.shape[1]
    for k in range(2):
        mine = pl.multiple_of((2 * k + core) * rows, 8)
        other = pl.multiple_of((2 * k + 1 - core) * rows, 8)
        send_ref[k] = acc_ref[pl.ds(other, rows), :].astype(BF16)
        keep_ref[k] = acc_ref[pl.ds(mine, rows), :].astype(BF16)


def text_head_kernel(core_ref, *refs):
    pairs, (keep_ref, send_ref, acc_ref) = refs[:-3], refs[-3:]
    total = None
    for i in range(0, len(pairs), 2):
        part = over_rows(pairs[i][...], pairs[i + 1][...])
        total = part if total is None else total + part
    acc_ref[...] = total
    part_by_core(core_ref[0], acc_ref, keep_ref, send_ref)


def text_head_part(core, *pairs):
    depth, wide = pairs[0].shape[1], pairs[1].shape[1]
    half = shape((2, depth // 4, wide), BF16)
    return local(
        text_head_kernel,
        [half, half],
        core,
        *pairs,
        scalars=1,
        scratch=[pltpu.VMEM((depth, wide), F32)],
        mib=20,
    )


def image_side_kernel(count, *refs):
    txt_refs, w_refs, first_ref, rest_ref = (
        refs[:count],
        refs[count : 2 * count - 1],
        refs[2 * count - 1],
        refs[2 * count],
    )
    keep_ref, send_ref = refs[-2:]
    for i in (1, 3, 0, 2):
        weights = [first_ref[i] if i < 2 else rest_ref[i - 2]] + [ref[i] for ref in w_refs]
        dz = None
        for w, txt_ref in zip(weights, txt_refs):
            part = over_rows(w, txt_ref[...])
            dz = part if dz is None else dz + part
        if i % 2 == 0:
            keep_ref[i // 2] = dz
        else:
            send_ref[i // 2] = dz.astype(BF16)


def image_side(txts, weights, home):
    rows, wide = txts[0].shape
    dims = (2, rows, wide)
    return local(
        functools.partial(image_side_kernel, len(txts)),
        [shape(dims, F32), shape(dims, BF16)],
        *txts,
        *weights,
        *home,
        mib=20,
    )


def image_head_kernel(core_ref, keep_ref, got_ref, *refs):
    zb_refs, inv_refs, feats_refs = refs[:2], refs[2:4], refs[4:6]
    own_ref, next_ref, left_ref, send_ref, acc_ref = refs[6:]
    total = None
    for i in (1, 0):
        dz = keep_ref[i] + got_ref[i].astype(F32)
        if i == 0:
            own_ref[...] = dz.astype(BF16)
        else:
            next_ref[...] = dz.astype(BF16)
        du = tangent(zb_refs[i][...].astype(F32), inv_refs[i][...], dz).astype(BF16)
        part = over_rows(feats_refs[i][...], du)
        total = part if total is None else total + part
    acc_ref[...] = total
    part_by_core(core_ref[0], acc_ref, left_ref, send_ref)


def image_head_part(core, keep, got, zbs, invs, feats):
    dims = keep.shape[1:]
    block = shape(dims, BF16)
    depth = feats[0].shape[1]
    half = shape((2, depth // 4, dims[1]), BF16)
    return local(
        image_head_kernel,
        [block, block, half, half],
        core,
        keep,
        got,
        *zbs,
        *invs,
        *feats,
        scalars=1,
        scratch=[pltpu.VMEM((depth, dims[1]), F32)],
        mib=24,
    )


def split_x_kernel(got_ref, keep_ref, out_ref):
    rows = out_ref.shape[1]
    for k in range(out_ref.shape[0]):
        at = pl.ds(k % 2 * rows, rows)
        out_ref[k] = (keep_ref[k // 2, at].astype(F32) + got_ref[k // 2, at].astype(F32)).astype(BF16)


def split_x(keep, got):
    _, rows, wide = keep.shape
    return local(split_x_kernel, shape((4, rows // 2, wide), BF16), got, keep)


def split_y_kernel(me_ref, got_ref, keep_ref, *refs):
    outs, held = refs[:-1], refs[-1]
    count, tall, _ = held.shape
    rows = tall // 4
    total = keep_ref[...].astype(F32) + got_ref[...].astype(F32)
    for k in range(count):
        at = [(b // 2, (b % 2 * count + k) * rows) for b in range(4)]
        held[k] = jnp.concatenate([total[h, r : r + rows] for h, r in at], axis=0).astype(BF16)
    for s, out_ref in enumerate(outs):
        out_ref[...] = held[lax.rem(me_ref[0] + s, count)]


def split_y(me, keep, got):
    count = lax.axis_size("y")
    _, rows, wide = keep.shape
    part = (2 * rows // count, wide)
    return local(
        split_y_kernel,
        [shape(part, BF16)] * count,
        me,
        got,
        keep,
        scalars=1,
        scratch=[pltpu.VMEM((count,) + part, BF16)],
    )


def sum_of(ref):
    total = ref[0].astype(F32)
    for k in range(1, ref.shape[0]):
        total = total + ref[k].astype(F32)
    return total


def sum_kernel(*refs):
    total = refs[0][...].astype(F32)
    for ref in refs[1:-1]:
        total = total + ref[...].astype(F32)
    out_ref = refs[-1]
    rows = out_ref.shape[1]
    for k in range(out_ref.shape[0]):
        out_ref[k] = total[k * rows : (k + 1) * rows].astype(BF16)


def add_up(*parts):
    rows, wide = parts[0].shape
    return local(sum_kernel, shape((4, rows // 4, wide), BF16), *parts)


def sum_split_y_kernel(in_ref, out_ref):
    total = sum_of(in_ref).astype(BF16)
    rows = out_ref.shape[1]
    for k in range(out_ref.shape[0]):
        out_ref[k] = total[k * rows : (k + 1) * rows]


def sum_split_y(parts):
    count = lax.axis_size("y")
    _, rows, wide = parts.shape
    return local(sum_split_y_kernel, shape((count, rows // count, wide), BF16), parts)


def split_z_kernel(img_ref, txt_ref, out_ref):
    both = jnp.concatenate([sum_of(img_ref), sum_of(txt_ref)], axis=0)
    cols = [both[:, at : at + 128] for at in range(0, both.shape[1], 128)]
    tall = jnp.concatenate(cols, axis=0)
    rows = out_ref.shape[1]
    for k in range(out_ref.shape[0]):
        out_ref[k] = tall[k * rows : (k + 1) * rows].astype(BF16)


def split_z(img, txt):
    count = lax.axis_size("z")
    _, rows, wide = img.shape
    dims = (count, 2 * rows * wide // 128 // count, 128)
    return local(split_z_kernel, shape(dims, BF16), img, txt)


def sum_spread_kernel(in_ref, out_ref):
    total = sum_of(in_ref).astype(BF16)
    for k in range(out_ref.shape[0]):
        out_ref[k] = total


def sum_spread(parts):
    return local(sum_spread_kernel, shape(parts.shape, BF16), parts)


def join_z_kernel(in_ref, out_ref):
    tall = jnp.concatenate([in_ref[k].astype(F32) for k in range(in_ref.shape[0])], axis=0)
    rows, wide = out_ref.shape[1:]
    cols = [tall[k * rows : (k + 1) * rows] for k in range(wide // 128)]
    both = jnp.concatenate(cols, axis=1).astype(BF16)
    for k in range(out_ref.shape[0]):
        out_ref[k] = both


def join_z(pieces, wide, copies):
    count, rows, lanes = pieces.shape
    return local(join_z_kernel, shape((copies, count * rows * lanes // wide, wide), BF16), pieces)


def finish_kernel(part, in_ref, out_ref):
    count, both, wide = in_ref.shape
    rows = both // 2
    for k in range(count):
        for j in range(2):
            out_ref[k * rows : (k + 1) * rows, j * wide : (j + 1) * wide] = (
                in_ref[k, j * rows : (j + 1) * rows].astype(F32) * part
            )


def finish(part, pieces):
    count, both, wide = pieces.shape
    return local(
        functools.partial(finish_kernel, part), shape((count * both // 2, 2 * wide), F32), pieces
    )


def grads_kernel(feats_ref, head_ref, *refs):
    parts, out_ref = refs[:-1], refs[-1]
    z, inv = embedding(feats_ref[...], head_ref[...])
    dz = parts[0][...].astype(F32)
    for ref in parts[1:]:
        dz = dz + ref[...].astype(F32)
    du = tangent(z, inv, dz).astype(BF16)
    out = lax.dot_general(du, head_ref[...], LANES_BOTH, preferred_element_type=F32)
    out_ref[...] = out.astype(BF16)


def feature_grads(feats, head, *parts):
    return local(grads_kernel, shape(feats.shape, BF16), feats, head, *parts)


def far_z(block):
    count = lax.axis_size("z")
    return lax.ppermute(block, "z", [(i, (i + count // 2) % count) for i in range(count)])


def along_y(parts):
    count = lax.axis_size("y")
    return [parts[0]] + [
        lax.ppermute(part, "y", [(i, (i + s) % count) for i in range(count)])
        for s, part in enumerate(parts)
        if s > 0
    ]


def swap(block, axes):
    return lax.all_to_all(block, axes, 0, 0, tiled=True)


def per_device(image_feats, text_feats, image_head, text_head, scale, bias):
    core = lax.axis_index("c").astype(jnp.int32).reshape(1)
    me_y = lax.axis_index("y").astype(jnp.int32).reshape(1)

    def unit(work):
        def nothing():
            return jax.tree.map(lambda s: jnp.zeros(s.shape, s.dtype), jax.eval_shape(work))

        return lax.cond(scale[0] > 0, work, nothing)

    far = far_z(text_feats)

    near = lax.ppermute(text_feats, X_RING, CROSS)
    next_feats = lax.ppermute(image_feats, "xl", SWAP)

    def own_unit():
        core_feats = lax.ppermute(image_feats, "c", SWAP)
        zb_img, late_img, inv_img = embed(image_head, image_feats)
        zb_core = embed_other(image_head, core_feats)
        zb_txt, inv_txt, w_first = home_first(
            scale, bias, text_feats, text_head, [zb_img, zb_core]
        )
        return zb_img, zb_core, late_img, inv_img, zb_txt, inv_txt, w_first

    zb_img, zb_core, late_img, inv_img, zb_txt, inv_txt, w_first = unit(own_unit)
    near, next_feats, w_first = lax.optimization_barrier((near, next_feats, w_first))

    def group_unit():
        next_core_feats = lax.ppermute(next_feats, "c", SWAP)
        zb_next, late_next, inv_next = embed(image_head, next_feats)
        zb_next_core = embed_other(image_head, next_core_feats)
        imgs = [zb_img, zb_core, zb_next, zb_next_core]
        w_rest, dz_txt, du_home, zb_near, w_near, back_near, du_near = group_block(
            scale, bias, zb_txt, inv_txt, w_first, near, text_head, imgs
        )
        return dict(
            imgs=imgs[2:],
            late=late_next,
            inv=inv_next,
            w_rest=w_rest,
            dz_txt=dz_txt,
            zb_near=zb_near,
            w_near=w_near,
            back_near=back_near,
            dus=[du_home, du_near],
        )

    got = unit(group_unit)
    far, dus = lax.optimization_barrier((far, got["dus"]))
    zb_far, w_far, back_far, du_far = text_block(
        scale, bias, far, text_head, [zb_img, zb_core] + got["imgs"]
    )
    back_far = far_z(back_far)
    keep_txt, send = text_head_part(core, far, du_far, text_feats, dus[0], near, dus[1])
    got_txt = lax.ppermute(send, "c", SWAP)
    keep_txt, w_far = lax.optimization_barrier((keep_txt, w_far))
    keep_dz, send_dz = image_side(
        [zb_txt, got["zb_near"], zb_far], [got["w_near"], w_far], [w_first, got["w_rest"]]
    )
    got_dz = lax.ppermute(send_dz, "c", SWAP)
    txt = split_x(keep_txt, got_txt)
    txt, got_dz = lax.optimization_barrier((txt, got_dz))
    txt = swap(txt, ("xl", "xh"))

    def image_unit():
        own, send, keep, part = image_head_part(
            core,
            keep_dz,
            got_dz,
            [late_img, got["late"]],
            [inv_img, got["inv"]],
            [image_feats, next_feats],
        )
        return own, send, split_y(me_y, keep, lax.ppermute(part, "c", SWAP))

    own, send, img = unit(image_unit)
    img = along_y(img)
    txt = swap(sum_split_y(txt), "y")
    txt, img = lax.optimization_barrier((txt, add_up(*img)))

    def second_unit():
        return split_z(swap(img, ("xl", "xh")), txt)

    piece, send, back_near = lax.optimization_barrier((unit(second_unit), send, got["back_near"]))
    back_img = lax.ppermute(send, "xl", SWAP)
    back_near = lax.ppermute(back_near, X_RING, CROSS)
    piece, back_far = lax.optimization_barrier((piece, back_far))
    piece = swap(piece, "z")
    piece, back_img, back_far, back_near = lax.optimization_barrier(
        (piece, back_img, back_far, back_near)
    )
    image_grads = feature_grads(image_feats, image_head, own, back_img)
    text_grads = feature_grads(text_feats, text_head, got["dz_txt"], back_near, back_far)

    piece = join_z(swap(sum_spread(piece), "z"), image_head.shape[1], lax.axis_size(("xh", "y")))
    parts = lax.axis_size(("xh", "z", "y")) * lax.axis_size(("xl", "c"))
    head_grads = finish(1.0 / parts, swap(piece, ("xh", "y")))
    return (image_grads, text_grads, head_grads)


def solution(mesh):
    fine = Mesh(mesh.devices.reshape(2, 8, 4, 2, 2), ROWS)
    split = P(ROWS, None)
    return jax.shard_map(
        per_device,
        mesh=fine,
        in_specs=(split, split, P(), P(), P(), P()),
        out_specs=(split, split, P(("xl", "c"), None)),
        check_vma=False,
    )
```
